512 devices in a mesh: gz: 16 (over z), pr: 4 (over y), pc: 8 (over x, core).
Axes of the slice: x: 4, y: 4, z: 16, core: 2. Of those that a mesh axis runs over, the one named last changes fastest.
Arguments:
- contributions: float32 [16, 8192, 4096], P('gz', 'pr', 'pc'), may hold values from -1.5 to 1.5
- pivot_inverses: float32 [4, 512, 512], P(None, ('gz', 'pr')), may hold values from -0.01171875 to 0.01171875
Outputs:
- factored: float32 [4, 2048, 4096], P('pr', 'gz', 'pc')
The draws below stay inside these ranges and needn't reach their ends.
All inputs are finite; a program needn't handle non-finite values.
Results may differ from the reference program's by a relative error of at most 0.00025.
Values sent between devices are 32-bit elements; how exact they have to be, the bound alone decides.
A program may use at most 64 MiB of HBM per device.

```python
import jax
import jax.numpy as jnp
from jax import lax

NB = 512
PANELS = 4
WIN_COLS = 4096
WIN_ROWS = 8192
LAYERS = 16
N_GZ = 16
N_PR = 4


def steps_of(key, shape, split, least, high):
    factor_of, own = 1.0, jax.random.fold_in(key, 6)
    for dim, shards_of in split:
        draws = jnp.exp(jax.random.uniform(jax.random.fold_in(own, dim), (shards_of,), jnp.float32, least / len(split), high / len(split)))
        factor_of = factor_of * jnp.repeat(draws, shape[dim] // shards_of).reshape([-1 if axis == dim else 1 for axis in range(len(shape))])
    return factor_of


def gaussian(own_key, shape, spread, most, shards=(), dtype=jnp.bfloat16):
    factor_of = steps_of(own_key, shape, shards, -0.22, 0.18) if shards else 1.0
    values = jax.random.normal(own_key, shape, jnp.float32) * spread * factor_of
    return jnp.minimum(jnp.maximum(values, -most), most).astype(dtype)


def setup_inputs(seed: int = 0) -> dict:
    keys = jax.random.split(jax.random.key(seed), 3)
    return {
        "contributions": gaussian(keys[0], (LAYERS, WIN_ROWS, WIN_COLS), N_GZ ** -0.5, 1.5, ((0, 16), (1, 4), (2, 8)), jnp.float32),
        "pivot_inverses": gaussian(keys[1], (PANELS, NB, NB), (NB * NB) ** -0.5, 0.01171875, ((1, 64),), jnp.float32),
    }


def reference(contributions, pivot_inverses):
    front_block = jnp.sum(contributions, axis=0)
    row_index = jnp.arange(WIN_ROWS)[:, None]
    col_index = jnp.arange(WIN_COLS)[None, :]
    for panel_idx in range(PANELS):
        start_col = panel_idx * NB
        end_col = start_col + NB
        multipliers = jnp.dot(front_block[:, start_col:end_col], pivot_inverses[panel_idx], precision=lax.Precision.HIGHEST, preferred_element_type=jnp.float32)
        multipliers = jnp.where(row_index >= end_col, multipliers, jnp.float32(0.0))
        pivot_rows = jnp.where(col_index >= end_col, front_block[start_col:end_col, :], jnp.float32(0.0))
        front_block = front_block - jnp.dot(multipliers, pivot_rows, precision=lax.Precision.HIGHEST, preferred_element_type=jnp.float32)
        kept_cols = jnp.where(row_index >= end_col, multipliers, front_block[:, start_col:end_col])
        front_block = front_block.at[:, start_col:end_col].set(kept_cols)
    return front_block.reshape(N_PR, WIN_ROWS // N_PR, WIN_COLS)
```

```python
import functools

import jax
import jax.numpy as jnp
from jax import lax
from jax.experimental import pallas as pl
from jax.experimental.pallas import tpu as pltpu
from jax.sharding import PartitionSpec as P

NB = 512
PANELS = 4
NZ, NY, NC = 16, 4, 8
SUB = 32
COLS = NB // NY
ROWS = 4 * SUB
MESH = pl.DeviceIdType.MESH


def split(value):
    high = value.astype(jnp.bfloat16)
    low = (value - high.astype(jnp.float32)).astype(jnp.bfloat16)
    return high, low


def dot3(value, high_ref, low_ref):
    high, low = split(value)
    mul = functools.partial(jnp.dot, preferred_element_type=jnp.float32)
    return mul(high, high_ref[...]) + (mul(high, low_ref[...]) + mul(low, high_ref[...]))


def kernel(
    contrib_in, inv_in, out, contrib, slots, front, tops, inv, piv, inv_hi, inv_lo, own_hi, own_lo,
    piv_hi, piv_lo, blocks, top_mult, mult, dealt,
    in_sem, rs_send, rs_recv, g_send, g_recv, y_send, y_recv, a_send, a_recv, m_send, m_recv, d_send, d_recv,
):
    z, y, c = lax.axis_index("gz"), lax.axis_index("pr"), lax.axis_index("pc")
    core, x = lax.rem(c, 2), c // 2
    sgn = 1 - 2 * core
    top = y == 0
    low_rows = y > 0
    zhi, zlo = z // 4, lax.rem(z, 4)
    none = y * 0

    def at_z(d):
        return lax.rem(z + d + NZ, NZ)

    def at_y(d):
        return lax.rem(y + d + NY, NY)

    load = pltpu.make_async_copy(contrib_in, contrib, in_sem.at[0])
    load.start()
    load_inv = pltpu.make_async_copy(inv_in.at[jnp.minimum(c, PANELS - 1)], inv.at[z, y], in_sem.at[1])
    load_inv.start()

    barrier = pltpu.get_barrier_semaphore()
    for d in (1, -1, 2, -2, 3, -3, 5, -5):
        pl.semaphore_signal(barrier, inc=1, device_id={"gz": at_z(d)}, device_id_type=MESH)
    for d in range(1, NY):
        pl.semaphore_signal(barrier, inc=1, device_id={"pr": at_y(d)}, device_id_type=MESH)
    for d in range(1, NC):
        pl.semaphore_signal(barrier, inc=1, device_id={"pc": lax.rem(c + d, NC)}, device_id_type=MESH)
    pl.semaphore_wait(barrier, 8 + NY - 1 + NC - 1)

    pending = []

    def send(parts, cond=None):
        def copy():
            src, dst, send_sem, recv_sem, device = parts()
            return pltpu.make_async_remote_copy(
                src_ref=src, dst_ref=dst, send_sem=send_sem, recv_sem=recv_sem,
                device_id=device, device_id_type=MESH,
            )

        copy().start()
        pending.append((cond, copy))

    def arrived(dst, send_sem, recv_sem, device):
        pltpu.make_async_remote_copy(
            src_ref=dst, dst_ref=dst, send_sem=send_sem, recv_sem=recv_sem,
            device_id=device, device_id_type=MESH,
        ).wait_recv()

    def rows_of(q, dest):
        first = jnp.where(top, NB * q + SUB * dest, ROWS * dest + SUB * q)
        return contrib.at[pl.ds(pl.multiple_of(first, SUB), SUB), :]

    hops = (8, 7)

    def rs_step(q, way, step):
        toward = sgn if way == 0 else -sgn
        total = hops[way]
        if step > 0:
            src = slots.at[q, way, step - 1]
            arrived(src, rs_send.at[q, way, step - 1], rs_recv.at[q, way, step - 1], {"gz": at_z(-toward)})
            if step < total:
                src[...] = src[...] + rows_of(q, at_z(toward * (total - step)))[...]
        if step < total:
            send(lambda: (
                slots.at[q, way, step - 1] if step > 0 else rows_of(q, at_z(toward * total)),
                slots.at[q, way, step], rs_send.at[q, way, step], rs_recv.at[q, way, step],
                {"gz": at_z(toward)},
            ))

    near = (1, -1, 2, -2)

    def hop(buf, g, at, piece, d):
        src = buf.at[at_z(piece), y]
        return src, src, g_send.at[g, at], g_recv.at[g, at], {"gz": at_z(d)}

    def landed(buf, g, at, piece, d):
        arrived(buf.at[at_z(piece), y], g_send.at[g, at], g_recv.at[g, at], {"gz": at_z(d)})

    def gather_start(buf, g, cond):
        for n, d in enumerate((5, -5)):
            send(functools.partial(hop, buf, g, n, 0, d), cond)
        for n, d in enumerate(near):
            send(functools.partial(hop, buf, g, 2 + n, 0, d), cond)

    def extra(buf, g):
        return hop(buf, g, 14, 5 * sgn, -3 * sgn)

    def gather_pass(buf, g, cond):
        for n, far in enumerate((-5, 5)):
            landed(buf, g, n, far, far)
            for m, d in enumerate(near):
                send(functools.partial(hop, buf, g, 6 + 4 * n + m, far, d), cond)
        send(functools.partial(extra, buf, g), cond)

    def gather_near(buf, g):
        for m, d in enumerate(near):
            landed(buf, g, 2 + m, -d, -d)
        for n, far in enumerate((-5, 5)):
            for m, d in enumerate(near):
                landed(buf, g, 6 + 4 * n + m, far - d, -d)
        landed(buf, g, 14, 8, 3 * sgn)

    def y_part(buf, g, at, half, of, d):
        src = buf.at[8 * half : 8 * half + 8, at_y(of)]
        return src, src, y_send.at[g, at], y_recv.at[g, at], {"pr": at_y(d)}

    def y_landed(buf, g, at, half, of, d):
        arrived(buf.at[8 * half : 8 * half + 8, at_y(of)], y_send.at[g, at], y_recv.at[g, at], {"pr": at_y(d)})

    def gather_y(buf, g, cond):
        for n in range(2):
            for way, d in enumerate((1, -1)):
                half = (n + way) % 2
                send(functools.partial(y_part, buf, g, 2 * way + half, half, 0, d), cond)

    def gather_y_pass(buf, g, cond):
        for n in range(2):
            for way, d in enumerate((1, -1)):
                half = (n + way) % 2
                y_landed(buf, g, 2 * way + half, half, -d, -d)
                if n == 0:
                    send(functools.partial(y_part, buf, g, 4 + way, half, -d, d), cond)

    def gather_y_end(buf, g):
        for way, d in enumerate((1, -1)):
            y_landed(buf, g, 4 + way, way, 2, -d)

    def has_inv():
        return c < PANELS

    load_inv.wait()
    load.wait()
    for step in range(9):
        for q in range(4):
            for way in range(2):
                if step <= hops[way]:
                    rs_step(q, way, step)
        if step == 0:
            pl.when(has_inv())(lambda: gather_start(inv, 0, has_inv))
        if step == 3:
            pl.when(has_inv())(lambda: gather_pass(inv, 0, has_inv))
        if step == 5:
            @pl.when(has_inv())
            def _():
                gather_near(inv, 0)
                gather_y(inv, 0, has_inv)
        if step == 7:
            pl.when(has_inv())(lambda: gather_y_pass(inv, 0, has_inv))
    for q in range(4):
        front[q] = rows_of(q, z)[...] + slots[q, 0, 7] + slots[q, 1, 6]

    def is_top():
        return y == 0

    def share(d):
        return (
            front.at[:, :, COLS * d : COLS * d + COLS], tops, a_send.at[d - 1], a_recv.at[0], {"pr": none + d},
        )

    @pl.when(is_top())
    def _():
        for d in range(1, NY):
            send(functools.partial(share, d), is_top)
        tops[...] = front[:, :, 0:COLS]

    @pl.when(has_inv())
    def _():
        gather_y_end(inv, 0)
        high, low = split(inv[...].reshape(NB, NB))
        inv_hi[...] = high
        inv_lo[...] = low

    @pl.when(low_rows)
    def _():
        arrived(tops, a_send.at[0], a_recv.at[0], {"pr": none})

    def deal_part(k):
        cols = pl.ds(pl.multiple_of(COLS * y, COLS), COLS)
        return (
            tops.at[k], dealt.at[zlo, :, cols], d_send.at[k], d_recv.at[zlo, y], {"gz": 4 * k + zhi, "pr": none},
        )

    def away(k):
        return jnp.logical_not(jnp.logical_and(y == 0, 4 * k + zhi == z))

    def deal(k):
        @pl.when(away(k))
        def _():
            send(functools.partial(deal_part, k), functools.partial(away, k))

        @pl.when(jnp.logical_not(away(k)))
        def _():
            dealt[zlo, :, 0:COLS] = tops[k]

    def owns(k):
        return c == k

    def right_of(k):
        return c > k

    def low_owns(k):
        return jnp.logical_and(c == k, y > 0)

    def peers_of(k):
        owner_x, owner_core = k // 2, k % 2
        same = [2 * n + owner_core for n in range(NC // 2) if n != owner_x and 2 * n + 1 > k]
        if owner_core == 0:
            same.append(k + 1)
        if k == 1:
            same.append(2)
        return same

    def mult_part(kind, k, n, peer):
        ref = mult.at[k] if kind else top_mult.at[k, k + 1 : 4]
        return ref, ref, m_send.at[kind, k, n], m_recv.at[kind, k], {"pc": none + peer}

    def mult_on(kind, k):
        ref = mult.at[k] if kind else top_mult.at[k, k + 1 : 4]
        return ref, ref, m_send.at[kind, k, 0], m_recv.at[kind, k], {"pc": 2 * x + 1 - core}

    def hands_on(kind, k):
        given = jnp.logical_and(core == k % 2, jnp.logical_and(x != k // 2, c > k))
        if k == 1:
            given = jnp.logical_and(given, c > 3)
        return jnp.logical_and(given, y > 0) if kind else given

    def mult_in(kind, k):
        ref, _, send_sem, recv_sem, device = mult_on(kind, k)
        arrived(ref, send_sem, recv_sem, device)

    def take_on(kind, k):
        @pl.when(hands_on(kind, k))
        def _():
            mult_in(kind, k)
            send(functools.partial(mult_on, kind, k), functools.partial(hands_on, kind, k))

    def wait_mult(kind, k):
        pl.when(jnp.logical_not(hands_on(kind, k)))(lambda: mult_in(kind, k))

    def block_part(k, d):
        ref = blocks.at[y, k + 1 : 4]
        return ref, ref, a_send.at[2 + d], a_recv.at[d], {"pr": at_y(d)}

    pivots = [piv.at[k] for k in range(PANELS)]

    def low_update(k):
        wait_mult(1, k)
        gather_y_end(pivots[k], k + 1)
        for n in range(NY):
            high, low = split(piv[k, :, n].reshape(NB, COLS))
            piv_hi[:, COLS * n : COLS * n + COLS] = high
            piv_lo[:, COLS * n : COLS * n + COLS] = low
        held = front[...].reshape(ROWS, NB)
        front[...] = (held - dot3(mult[k], piv_hi, piv_lo)).reshape(4, SUB, NB)

    def panel(k):
        g = k + 1
        right = functools.partial(right_of, k)
        mine = functools.partial(owns, k)
        left = 3 - k

        @pl.when(right())
        def _():
            piv[k, z, y] = tops[k]
            gather_start(pivots[k], g, right)

        if k < 3:
            @pl.when(mine())
            def _():
                blocks[y, k + 1 : 4] = tops[k + 1 : 4]
                for d in range(1, NY):
                    send(functools.partial(block_part, k, d), mine)

        deal(k)
        if k >= 2:
            @pl.when(jnp.logical_and(c >= k, low_rows))
            def _():
                low_update(k - 2)

        @pl.when(right())
        def _():
            gather_pass(pivots[k], g, right)

        if k < 3:
            @pl.when(mine())
            def _():
                for d in range(1, NY):
                    arrived(blocks.at[at_y(-d), k + 1 : 4], a_send.at[2 + d], a_recv.at[d], {"pr": at_y(-d)})
                whole = jnp.concatenate([blocks[n, k + 1 : 4].reshape(left * SUB, COLS) for n in range(NY)], axis=1)
                top_mult[k, k + 1 : 4] = dot3(whole, inv_hi, inv_lo).reshape(left, SUB, NB)
                for n, peer in enumerate(peers_of(k)):
                    send(functools.partial(mult_part, 0, k, n, peer), mine)
                cols = pl.ds(pl.multiple_of(COLS * y, COLS), COLS)
                tops[k + 1 : 4] = top_mult[k, k + 1 : 4, :, cols]

        if k >= 1:
            @pl.when(right_of(k - 1))
            def _():
                gather_y_pass(pivots[k - 1], g - 1, functools.partial(right_of, k - 1))

            @pl.when(jnp.logical_and(mine(), low_rows))
            def _():
                low_update(k - 1)

        @pl.when(low_owns(k))
        def _():
            product = dot3(front[...].reshape(ROWS, NB), inv_hi, inv_lo)
            mult[k] = product
            for n, peer in enumerate(peers_of(k)):
                send(functools.partial(mult_part, 1, k, n, peer), functools.partial(low_owns, k))

        @pl.when(right())
        def _():
            if k < 3:
                take_on(0, k)
                wait_mult(0, k)
            gather_near(pivots[k], g)
            gather_y(pivots[k], g, right)
            if k < 3:
                high, low = split(piv[k, :, y].reshape(NB, COLS))
                own_hi[...] = high
                own_lo[...] = low
                product = dot3(top_mult[k, k + 1 : 4].reshape(left * SUB, NB), own_hi, own_lo)
                tops[k + 1 : 4] = tops[k + 1 : 4] - product.reshape(left, SUB, COLS)

        if k >= 1:
            take_on(1, k - 1)

    for k in range(PANELS):
        panel(k)

    last = PANELS - 1

    @pl.when(right_of(last))
    def _():
        gather_y_pass(pivots[last], last + 1, functools.partial(right_of, last))

        pl.when(low_rows)(lambda: low_update(last - 1))
        take_on(1, last)
        pl.when(low_rows)(lambda: low_update(last))

    @pl.when(top)
    def _():
        for k in range(PANELS):
            @pl.when(right_of(k))
            def _():
                gather_y_end(pivots[k], k + 1)

    @pl.when(is_top())
    def _():
        for n in range(4):
            for m in range(NY):
                def from_far():
                    cols = slice(COLS * m, COLS * m + COLS)
                    arrived(dealt.at[n, :, cols], d_send.at[0], d_recv.at[n, m], {"gz": 4 * zlo + n, "pr": none + m})

                if m == 0:
                    pl.when(4 * zlo + n != z)(from_far)
                else:
                    from_far()
        out[...] = dealt[...].reshape(ROWS, NB)

    @pl.when(low_rows)
    def _():
        out[...] = front[...].reshape(ROWS, NB)

        for k in range(PANELS):
            @pl.when(owns(k))
            def _():
                out[...] = mult[k]

    for cond, copy in pending:
        if cond is None:
            copy().wait_send()
        else:
            pl.when(cond())(lambda: copy().wait_send())


def shards(contributions, pivot_inverses):
    f32, bf16 = jnp.float32, jnp.bfloat16
    dma = pltpu.SemaphoreType.DMA
    factored = pl.pallas_call(
        kernel,
        out_shape=jax.ShapeDtypeStruct((ROWS, NB), f32),
        in_specs=[pl.BlockSpec(memory_space=pl.ANY)] * 2,
        out_specs=pl.BlockSpec(memory_space=pltpu.VMEM),
        scratch_shapes=[
            pltpu.VMEM((NZ * ROWS, NB), f32),
            pltpu.VMEM((4, 2, 8, SUB, NB), f32),
            pltpu.VMEM((4, SUB, NB), f32),
            pltpu.VMEM((4, SUB, COLS), f32),
            pltpu.VMEM((NZ, NY, 8, NB), f32),
            pltpu.VMEM((PANELS, NZ, NY, SUB, COLS), f32),
            pltpu.VMEM((NB, NB), bf16),
            pltpu.VMEM((NB, NB), bf16),
            pltpu.VMEM((NB, COLS), bf16),
            pltpu.VMEM((NB, COLS), bf16),
            pltpu.VMEM((NB, NB), bf16),
            pltpu.VMEM((NB, NB), bf16),
            pltpu.VMEM((NY, 4, SUB, COLS), f32),
            pltpu.VMEM((PANELS, 4, SUB, NB), f32),
            pltpu.VMEM((PANELS, ROWS, NB), f32),
            pltpu.VMEM((4, SUB, NB), f32),
            dma((2,)),
            dma((4, 2, 8)),
            dma((4, 2, 8)),
            dma((PANELS + 1, 15)),
            dma((PANELS + 1, 15)),
            dma((PANELS + 1, 6)),
            dma((PANELS + 1, 6)),
            dma((6,)),
            dma((4,)),
            dma((2, PANELS, 5)),
            dma((2, PANELS)),
            dma((PANELS,)),
            dma((4, NY)),
        ],
        compiler_params=pltpu.CompilerParams(
            collective_id=0, has_side_effects=True, vmem_limit_bytes=56 * 1024 * 1024
        ),
    )(contributions[0], pivot_inverses)
    return factored[None]


def solution(mesh):
    placed = (P("gz", "pr", "pc"), P(None, ("gz", "pr"), None))
    return jax.shard_map(
        shards, mesh=mesh, in_specs=placed, out_specs=P("pr", "gz", "pc"), check_vma=False
    )
```

```python
import functools

import jax
import jax.numpy as jnp
from jax import lax
from jax.experimental import pallas as pl
from jax.experimental.pallas import tpu as pltpu
from jax.sharding import PartitionSpec as P

NB = 512
PANELS = 4
NZ, NY, NC = 16, 4, 8
SUB = 32
COLS = NB // NY
ROWS = 4 * SUB
MESH = pl.DeviceIdType.MESH


def split(value):
    high = value.astype(jnp.bfloat16)
    low = (value - high.astype(jnp.float32)).astype(jnp.bfloat16)
    return high, low


def dot3(value, high_ref, low_ref):
    high, low = split(value)
    mul = functools.partial(jnp.dot, preferred_element_type=jnp.float32)
    return mul(high, high_ref[...]) + (mul(high, low_ref[...]) + mul(low, high_ref[...]))


def kernel(
    contrib_in, inv_in, out, contrib, slots, front, tops, inv, piv, inv_hi, inv_lo, own_hi, own_lo,
    piv_hi, piv_lo, blocks, top_mult, mult, dealt,
    in_sem, rs_send, rs_recv, i_send, i_recv, iy_send, iy_recv, g_send, g_recv, py_send, py_recv, a_send, a_recv, m_send, m_recv, d_send, d_recv,
):
    z, y, c = lax.axis_index("gz"), lax.axis_index("pr"), lax.axis_index("pc")
    core, x = lax.rem(c, 2), c // 2
    sgn = 1 - 2 * core
    top = y == 0
    low_rows = y > 0
    zhi, zlo = z // 4, lax.rem(z, 4)
    none = y * 0

    def at_z(d):
        return lax.rem(z + d + NZ, NZ)

    def at_y(d):
        return lax.rem(y + d + NY, NY)

    load = pltpu.make_async_copy(contrib_in, contrib, in_sem.at[0])
    load.start()
    load_inv = pltpu.make_async_copy(inv_in.at[jnp.minimum(c, PANELS - 1)], inv.at[0, y], in_sem.at[1])
    load_inv.start()

    barrier = pltpu.get_barrier_semaphore()
    for d in (1, -1, 2, -2, 3, -3, 5, -5):
        pl.semaphore_signal(barrier, inc=1, device_id={"gz": at_z(d)}, device_id_type=MESH)
    for d in range(1, NY):
        pl.semaphore_signal(barrier, inc=1, device_id={"pr": at_y(d)}, device_id_type=MESH)
    for d in range(1, NC):
        pl.semaphore_signal(barrier, inc=1, device_id={"pc": lax.rem(c + d, NC)}, device_id_type=MESH)
    pl.semaphore_wait(barrier, 8 + NY - 1 + NC - 1)

    pending = []

    def send(parts, cond=None):
        def copy():
            src, dst, send_sem, recv_sem, device = parts()
            return pltpu.make_async_remote_copy(
                src_ref=src, dst_ref=dst, send_sem=send_sem, recv_sem=recv_sem,
                device_id=device, device_id_type=MESH,
            )

        copy().start()
        pending.append((cond, copy))

    def arrived(dst, send_sem, recv_sem, device):
        pltpu.make_async_remote_copy(
            src_ref=dst, dst_ref=dst, send_sem=send_sem, recv_sem=recv_sem,
            device_id=device, device_id_type=MESH,
        ).wait_recv()

    def rows_of(q, dest, ref=contrib):
        first = jnp.where(top, NB * q + SUB * dest, ROWS * dest + SUB * q)
        return ref.at[pl.ds(pl.multiple_of(first, SUB), SUB), :]

    hops = (8, 7)

    def rs_step(q, way, step):
        toward = sgn if way == 0 else -sgn
        total = hops[way]
        if step > 0:
            src = slots.at[q, way, step - 1]
            arrived(src, rs_send.at[q, way, step - 1], rs_recv.at[q, way, step - 1], {"gz": at_z(-toward)})
            if step < total:
                src[...] = src[...] + rows_of(q, at_z(toward * (total - step)))[...]
        if step < total:
            send(lambda: (
                slots.at[q, way, step - 1] if step > 0 else rows_of(q, at_z(toward * total), contrib_in),
                slots.at[q, way, step], rs_send.at[q, way, step], rs_recv.at[q, way, step],
                {"gz": at_z(toward)},
            ))

    def has_inv():
        return c < PANELS

    def ring_slot(way, step):
        return 0 if step == 0 else 2 * step - 1 + way

    def ring_part(way, step):
        toward = sgn if way == 0 else -sgn
        return (
            inv.at[ring_slot(way, step), y], inv.at[ring_slot(way, step + 1), y],
            i_send.at[way, step], i_recv.at[way, step], {"gz": at_z(toward)},
        )

    def ring_step(way, step):
        if step > 0:
            _, dst, send_sem, recv_sem, device = ring_part(way, step - 1)
            arrived(dst, send_sem, recv_sem, device)
        if step < hops[way]:
            send(functools.partial(ring_part, way, step), has_inv)

    def y_part(buf, chunk, send_sems, recv_sems, at, of, d):
        src = buf.at[chunk[0] : chunk[1], at_y(of)]
        return src, src, send_sems.at[at], recv_sems.at[at], {"pr": at_y(d)}

    def y_send(buf, chunks, send_sems, recv_sems, some, cond):
        for n in some:
            for way, d in ((0, 1), (1, -1)) if n % 2 == 0 else ((1, -1), (0, 1)):
                send(functools.partial(y_part, buf, chunks[n], send_sems, recv_sems, 3 * n + way, 0, d), cond)

    def y_landed(buf, chunks, send_sems, recv_sems, n, at, of, d):
        src, _, send_sem, recv_sem, device = y_part(buf, chunks[n], send_sems, recv_sems, at, of, -d)
        arrived(src, send_sem, recv_sem, device)

    def y_pass(buf, chunks, send_sems, recv_sems, some, cond):
        for n in some:
            d = 1 - 2 * (n % 2)
            y_landed(buf, chunks, send_sems, recv_sems, n, 3 * n + n % 2, -d, d)
            send(functools.partial(y_part, buf, chunks[n], send_sems, recv_sems, 3 * n + 2, -d, d), cond)

    def y_end_near(buf, chunks, send_sems, recv_sems):
        for n in range(len(chunks)):
            d = 1 - 2 * (n % 2)
            y_landed(buf, chunks, send_sems, recv_sems, n, 3 * n + 1 - n % 2, d, -d)

    def y_end_far(buf, chunks, send_sems, recv_sems):
        for n in range(len(chunks)):
            d = 1 - 2 * (n % 2)
            y_landed(buf, chunks, send_sems, recv_sems, n, 3 * n + 2, 2, d)

    def y_end(*gather):
        y_end_near(*gather)
        y_end_far(*gather)

    inv_chunks = ((0, 4), (4, 8), (8, 10), (10, 12), (12, 14), (14, 16))
    inv_y = (inv, inv_chunks, iy_send, iy_recv)

    near = (1, -1, 2, -2)
    order = (0, 1, -1, 2, -2, 5, -5, 6, 4, 7, 3, -6, -4, -7, -3, 8)
    chunks = ((0, 4), (4, 7), (7, 11), (11, 16))

    def hop(k, at, piece, d):
        return (
            piv.at[k, order.index(piece), y], piv.at[k, order.index(piece - d), y],
            g_send.at[k, at], g_recv.at[k, at], {"gz": at_z(d)},
        )

    def landed(k, at, piece, d):
        _, dst, send_sem, recv_sem, device = hop(k, at, piece, d)
        arrived(dst, send_sem, recv_sem, device)

    def piv_y(k):
        return pivots[k], chunks, y_sends[k], y_recvs[k]

    def gather_start(k, cond):
        for n, d in enumerate((5, -5)):
            send(functools.partial(hop, k, n, 0, d), cond)
        for n, d in enumerate(near):
            send(functools.partial(hop, k, 2 + n, 0, d), cond)

    def extra(k):
        return piv.at[k, 5 + core, y], piv.at[k, 15, y], g_send.at[k, 14], g_recv.at[k, 14], {"gz": at_z(-3 * sgn)}

    def gather_pass(k, cond):
        for n, d in enumerate((5, -5)):
            landed(k, n, 0, d)
            for m, e in enumerate(near):
                send(functools.partial(hop, k, 6 + 4 * n + m, -d, e), cond)
        send(functools.partial(extra, k), cond)
        for m, d in enumerate(near):
            landed(k, 2 + m, 0, d)
        y_send(*piv_y(k), (0, 1), cond)

    def gather_near(k, cond):
        for n, d in enumerate((5, -5)):
            for m, e in enumerate(near):
                landed(k, 6 + 4 * n + m, -d, e)
        _, dst, send_sem, recv_sem, device = extra(k)
        arrived(dst, send_sem, recv_sem, device)
        y_send(*piv_y(k), (2, 3), cond)

    def in_rows(j):
        return pl.ds(pl.multiple_of(SUB * at_z(order[j]), SUB), SUB)

    pivots = [piv.at[k] for k in range(PANELS)]
    y_sends = [py_send.at[k] for k in range(PANELS)]
    y_recvs = [py_recv.at[k] for k in range(PANELS)]

    for step in range(9):
        if step == 0:
            load_inv.wait()
        if step == 1:
            load.wait()
        for q in range(4):
            for way in range(2):
                if step <= hops[way]:
                    rs_step(q, way, step)

        @pl.when(has_inv())
        def _():
            for way in range(2):
                if step <= hops[way]:
                    ring_step(way, step)
            if step == 4:
                y_send(*inv_y, (0, 1), has_inv)
            if step == 6:
                y_pass(*inv_y, (0, 1), has_inv)
                y_send(*inv_y, (2, 3), has_inv)
            if step == 8:
                y_send(*inv_y, (4, 5), has_inv)
    for q in range(4):
        front[q] = rows_of(q, z)[...] + slots[q, 0, 7] + slots[q, 1, 6]

    def is_top():
        return y == 0

    def share(d):
        return (
            front.at[:, :, COLS * d : COLS * d + COLS], tops, a_send.at[d - 1], a_recv.at[0], {"pr": none + d},
        )

    @pl.when(is_top())
    def _():
        for d in range(1, NY):
            send(functools.partial(share, d), is_top)
        tops[...] = front[:, :, 0:COLS]

    @pl.when(has_inv())
    def _():
        y_pass(*inv_y, (2, 3, 4, 5), has_inv)

    @pl.when(low_rows)
    def _():
        arrived(tops, a_send.at[0], a_recv.at[0], {"pr": none})

    def deal_part(k):
        cols = pl.ds(pl.multiple_of(COLS * y, COLS), COLS)
        return (
            tops.at[k], dealt.at[zlo, :, cols], d_send.at[k], d_recv.at[zlo, y], {"gz": 4 * k + zhi, "pr": none},
        )

    def away(k):
        return jnp.logical_not(jnp.logical_and(y == 0, 4 * k + zhi == z))

    def deal(k):
        @pl.when(away(k))
        def _():
            send(functools.partial(deal_part, k), functools.partial(away, k))

        @pl.when(jnp.logical_not(away(k)))
        def _():
            dealt[zlo, :, 0:COLS] = tops[k]

    def owns(k):
        return c == k

    def right_of(k):
        return c > k

    def low_owns(k):
        return jnp.logical_and(c == k, y > 0)

    def peers_of(k):
        owner_x, owner_core = k // 2, k % 2
        same = [2 * n + owner_core for n in range(NC // 2) if n != owner_x and 2 * n + 1 > k]
        same[:2] = same[1::-1]
        if owner_core == 0:
            same.append(k + 1)
        if k == 1:
            same.append(2)
        return same

    def mult_ref(kind, k):
        if kind == 1:
            return mult.at[k]
        return top_mult.at[k, k + 2 : 4] if kind else top_mult.at[k, k + 1 : k + 2]

    def mult_part(kind, k, n, peer):
        ref = mult_ref(kind, k)
        return ref, ref, m_send.at[kind, k, n], m_recv.at[kind, k], {"pc": none + peer}

    def mult_on(kind, k):
        ref = mult_ref(kind, k)
        return ref, ref, m_send.at[kind, k, 0], m_recv.at[kind, k], {"pc": 2 * x + 1 - core}

    def hands_on(kind, k):
        given = jnp.logical_and(core == k % 2, jnp.logical_and(x != k // 2, c > k))
        if k == 1:
            given = jnp.logical_and(given, c > 3)
        return jnp.logical_and(given, y > 0) if kind == 1 else given

    def mult_in(kind, k):
        ref, _, send_sem, recv_sem, device = mult_on(kind, k)
        arrived(ref, send_sem, recv_sem, device)

    def take_on(kind, k):
        @pl.when(hands_on(kind, k))
        def _():
            mult_in(kind, k)
            send(functools.partial(mult_on, kind, k), functools.partial(hands_on, kind, k))

    def wait_mult(kind, k):
        pl.when(jnp.logical_not(hands_on(kind, k)))(lambda: mult_in(kind, k))

    def block_part(k, d):
        ref = blocks.at[y, k + 1 : 4]
        return ref, ref, a_send.at[2 + d], a_recv.at[d], {"pr": at_y(d)}

    def low_update(k, passing=False):
        def convert(m, d):
            for j in range(NZ):
                high, low = split(piv[k, j, at_y(d)])
                piv_hi[in_rows(j), COLS * m : COLS * m + COLS] = high
                piv_lo[in_rows(j), COLS * m : COLS * m + COLS] = low

        def subtract(m, pair):
            cols = slice(COLS * m, COLS * m + 2 * COLS)
            product = dot3(mult[k], piv_hi.at[:, cols], piv_lo.at[:, cols])
            for n, d in enumerate(pair):
                there = pl.ds(pl.multiple_of(COLS * at_y(d), COLS), COLS)
                part = product[:, COLS * n : COLS * n + COLS].reshape(4, SUB, COLS)
                front[:, :, there] = front[:, :, there] - part

        convert(0, 0)
        y_end_near(*piv_y(k))
        convert(1, 1)
        convert(2, -1)
        if passing:
            take_on(1, k)
        wait_mult(1, k)
        subtract(0, (0, 1))
        y_end_far(*piv_y(k))
        convert(3, 2)
        subtract(2, (-1, 2))

    def start(k):
        @pl.when(right_of(k))
        def _():
            piv[k, 0, y] = tops[k]
            gather_start(k, functools.partial(right_of, k))

    def exchange(k):
        @pl.when(owns(k))
        def _():
            blocks[y, k + 1 : 4] = tops[k + 1 : 4]
            for d in range(1, NY):
                send(functools.partial(block_part, k, d), functools.partial(owns, k))

    def top_update(k, first, end):
        rows = (end - first) * SUB
        product = dot3(top_mult[k, first:end].reshape(rows, NB), own_hi, own_lo)
        tops[first:end] = tops[first:end] - product.reshape(end - first, SUB, COLS)

    def panel(k):
        right = functools.partial(right_of, k)
        mine = functools.partial(owns, k)
        left = 3 - k

        if k >= 2:
            @pl.when(jnp.logical_and(c >= k, low_rows))
            def _():
                low_update(k - 2)

        pl.when(right())(lambda: gather_pass(k, right))
        deal(k)

        if k == 0:
            @pl.when(has_inv())
            def _():
                y_end(*inv_y)
                for way in range(2):
                    for step in range(way, hops[way] + 1):
                        source = at_z(sgn * (step if way else -step))
                        high, low = split(inv[ring_slot(way, step)].reshape(NY * 8, NB))
                        rows = pl.ds(pl.multiple_of(SUB * source, SUB), SUB)
                        inv_hi[rows, :] = high
                        inv_lo[rows, :] = low

        if k < 3:
            @pl.when(mine())
            def _():
                for d in range(1, NY):
                    arrived(blocks.at[at_y(-d), k + 1 : 4], a_send.at[2 + d], a_recv.at[d], {"pr": at_y(-d)})
                whole = jnp.concatenate([blocks[n, k + 1 : 4].reshape(left * SUB, COLS) for n in range(NY)], axis=1)
                top_mult[k, k + 1 : 4] = dot3(whole, inv_hi, inv_lo).reshape(left, SUB, NB)
                for kind in (0, 2) if k < 2 else (0,):
                    for n, peer in enumerate(peers_of(k)):
                        send(functools.partial(mult_part, kind, k, n, peer), mine)
                cols = pl.ds(pl.multiple_of(COLS * y, COLS), COLS)
                tops[k + 1 : 4] = top_mult[k, k + 1 : 4, :, cols]

        if k >= 1:
            @pl.when(right_of(k - 1))
            def _():
                y_pass(*piv_y(k - 1), range(4), functools.partial(right_of, k - 1))

            pl.when(low_owns(k))(lambda: low_update(k - 1))

        @pl.when(low_owns(k))
        def _():
            product = dot3(front[...].reshape(ROWS, NB), inv_hi, inv_lo)
            mult[k] = product
            for n, peer in enumerate(peers_of(k)):
                send(functools.partial(mult_part, 1, k, n, peer), functools.partial(low_owns, k))

        @pl.when(right())
        def _():
            if k < 3:
                take_on(0, k)
            if k == 3:
                take_on(1, k - 1)
            gather_near(k, right)
            if k == 3:
                y_pass(*piv_y(k), (0, 1), right)
                pl.when(low_rows)(lambda: low_update(k - 1))
            if k < 3:
                for j in range(NZ):
                    high, low = split(piv[k, j, y])
                    own_hi[in_rows(j), :] = high
                    own_lo[in_rows(j), :] = low
                wait_mult(0, k)
                top_update(k, k + 1, k + 2)

        if k < 3:
            start(k + 1)
        if k < 2:
            @pl.when(right())
            def _():
                take_on(2, k)
                wait_mult(2, k)
                top_update(k, k + 2, 4)

            exchange(k + 1)

        if k == 1 or k == 2:
            take_on(1, k - 1)

    start(0)
    exchange(0)
    for k in range(PANELS):
        panel(k)

    last = PANELS - 1

    @pl.when(right_of(last))
    def _():
        y_pass(*piv_y(last), (2, 3), functools.partial(right_of, last))
        pl.when(low_rows)(lambda: low_update(last, True))

    @pl.when(top)
    def _():
        for k in range(PANELS):
            @pl.when(right_of(k))
            def _():
                y_end(*piv_y(k))

    @pl.when(is_top())
    def _():
        for n in range(4):
            for m in range(NY):
                def from_far():
                    cols = slice(COLS * m, COLS * m + COLS)
                    arrived(dealt.at[n, :, cols], d_send.at[0], d_recv.at[n, m], {"gz": 4 * zlo + n, "pr": none + m})

                if m == 0:
                    pl.when(4 * zlo + n != z)(from_far)
                else:
                    from_far()
        out[...] = dealt[...].reshape(ROWS, NB)

    @pl.when(low_rows)
    def _():
        out[...] = front[...].reshape(ROWS, NB)

        for k in range(PANELS):
            @pl.when(owns(k))
            def _():
                out[...] = mult[k]

    for cond, copy in pending:
        if cond is None:
            copy().wait_send()
        else:
            pl.when(cond())(lambda: copy().wait_send())


def shards(contributions, pivot_inverses):
    f32, bf16 = jnp.float32, jnp.bfloat16
    dma = pltpu.SemaphoreType.DMA
    factored = pl.pallas_call(
        kernel,
        out_shape=jax.ShapeDtypeStruct((ROWS, NB), f32),
        in_specs=[pl.BlockSpec(memory_space=pl.ANY)] * 2,
        out_specs=pl.BlockSpec(memory_space=pltpu.VMEM),
        scratch_shapes=[
            pltpu.VMEM((NZ * ROWS, NB), f32),
            pltpu.VMEM((4, 2, 8, SUB, NB), f32),
            pltpu.VMEM((4, SUB, NB), f32),
            pltpu.VMEM((4, SUB, COLS), f32),
            pltpu.VMEM((NZ, NY, 8, NB), f32),
            pltpu.VMEM((PANELS, NZ, NY, SUB, COLS), f32),
            pltpu.VMEM((NB, NB), bf16),
            pltpu.VMEM((NB, NB), bf16),
            pltpu.VMEM((NB, COLS), bf16),
            pltpu.VMEM((NB, COLS), bf16),
            pltpu.VMEM((NB, NB), bf16),
            pltpu.VMEM((NB, NB), bf16),
            pltpu.VMEM((NY, 4, SUB, COLS), f32),
            pltpu.VMEM((PANELS, 4, SUB, NB), f32),
            pltpu.VMEM((PANELS, ROWS, NB), f32),
            pltpu.VMEM((4, SUB, NB), f32),
            dma((2,)),
            dma((4, 2, 8)),
            dma((4, 2, 8)),
            dma((2, 8)),
            dma((2, 8)),
            dma((18,)),
            dma((18,)),
            dma((PANELS, 15)),
            dma((PANELS, 15)),
            dma((PANELS, 12)),
            dma((PANELS, 12)),
            dma((6,)),
            dma((4,)),
            dma((3, PANELS, 5)),
            dma((3, PANELS)),
            dma((PANELS,)),
            dma((4, NY)),
        ],
        compiler_params=pltpu.CompilerParams(
            collective_id=0, has_side_effects=True, vmem_limit_bytes=56 * 1024 * 1024
        ),
    )(contributions[0], pivot_inverses)
    return factored[None]


def solution(mesh):
    placed = (P("gz", "pr", "pc"), P(None, ("gz", "pr"), None))
    return jax.shard_map(
        shards, mesh=mesh, in_specs=placed, out_specs=P("pr", "gz", "pc"), check_vma=False
    )
```

```python
import functools

import jax
import jax.numpy as jnp
from jax import lax
from jax.experimental import pallas as pl
from jax.experimental.pallas import tpu as pltpu
from jax.sharding import PartitionSpec as P

NB = 512
PANELS = 4
NZ, NY, NC = 16, 4, 8
SUB = 32
COLS = NB // NY
ROWS = 4 * SUB
MESH = pl.DeviceIdType.MESH


def split(value):
    high = value.astype(jnp.bfloat16)
    low = (value - high.astype(jnp.float32)).astype(jnp.bfloat16)
    return high, low


def dot3(value, high_ref, low_ref):
    high, low = split(value)
    mul = functools.partial(jnp.dot, preferred_element_type=jnp.float32)
    return mul(high, high_ref[...]) + (mul(high, low_ref[...]) + mul(low, high_ref[...]))


def kernel(
    contrib_in, inv_in, out, contrib, slots, front, tops, inv, piv, inv_hi, inv_lo, own_hi, own_lo,
    piv_hi, piv_lo, blocks, top_mult, mult, dealt,
    in_sem, rs_send, rs_recv, i_send, i_recv, iy_send, iy_recv, g_send, g_recv, py_send, py_recv, a_send, a_recv, m_send, m_recv, d_send, d_recv,
):
    z, y, c = lax.axis_index("gz"), lax.axis_index("pr"), lax.axis_index("pc")
    core, x = lax.rem(c, 2), c // 2
    sgn = 1 - 2 * core
    top = y == 0
    low_rows = y > 0
    zhi, zlo = z // 4, lax.rem(z, 4)
    none = y * 0

    def at_z(d):
        return lax.rem(z + d + NZ, NZ)

    def at_y(d):
        return lax.rem(y + d + NY, NY)

    load = pltpu.make_async_copy(contrib_in, contrib, in_sem.at[0])
    load.start()
    load_inv = pltpu.make_async_copy(inv_in.at[jnp.minimum(c, PANELS - 1)], inv.at[0, y], in_sem.at[1])
    load_inv.start()

    barrier = pltpu.get_barrier_semaphore()
    for d in (1, -1, 2, -2, 3, -3, 5, -5):
        pl.semaphore_signal(barrier, inc=1, device_id={"gz": at_z(d)}, device_id_type=MESH)
    for d in range(1, NY):
        pl.semaphore_signal(barrier, inc=1, device_id={"pr": at_y(d)}, device_id_type=MESH)
    for d in range(1, NC):
        pl.semaphore_signal(barrier, inc=1, device_id={"pc": lax.rem(c + d, NC)}, device_id_type=MESH)
    pl.semaphore_wait(barrier, 8 + NY - 1 + NC - 1)

    pending = []

    def send(parts, cond=None):
        def copy():
            src, dst, send_sem, recv_sem, device = parts()
            return pltpu.make_async_remote_copy(
                src_ref=src, dst_ref=dst, send_sem=send_sem, recv_sem=recv_sem,
                device_id=device, device_id_type=MESH,
            )

        copy().start()
        pending.append((cond, copy))

    def arrived(dst, send_sem, recv_sem, device):
        pltpu.make_async_remote_copy(
            src_ref=dst, dst_ref=dst, send_sem=send_sem, recv_sem=recv_sem,
            device_id=device, device_id_type=MESH,
        ).wait_recv()

    def rows_of(q, dest, ref=contrib):
        first = jnp.where(top, NB * q + SUB * dest, ROWS * dest + SUB * q)
        return ref.at[pl.ds(pl.multiple_of(first, SUB), SUB), :]

    hops = (8, 7)

    def rs_step(q, way, step):
        toward = sgn if way == 0 else -sgn
        total = hops[way]
        if step > 0:
            src = slots.at[q, way, step - 1]
            arrived(src, rs_send.at[q, way, step - 1], rs_recv.at[q, way, step - 1], {"gz": at_z(-toward)})
            if step < total:
                src[...] = src[...] + rows_of(q, at_z(toward * (total - step)))[...]
        if step < total:
            send(lambda: (
                slots.at[q, way, step - 1] if step > 0 else rows_of(q, at_z(toward * total), contrib_in),
                slots.at[q, way, step], rs_send.at[q, way, step], rs_recv.at[q, way, step],
                {"gz": at_z(toward)},
            ))

    def has_inv():
        return c < PANELS

    def ring_slot(way, step):
        return 0 if step == 0 else 2 * step - 1 + way

    def ring_part(way, step):
        toward = sgn if way == 0 else -sgn
        return (
            inv.at[ring_slot(way, step), y], inv.at[ring_slot(way, step + 1), y],
            i_send.at[way, step], i_recv.at[way, step], {"gz": at_z(toward)},
        )

    def ring_step(way, step):
        if step > 0:
            _, dst, send_sem, recv_sem, device = ring_part(way, step - 1)
            arrived(dst, send_sem, recv_sem, device)
        if step < hops[way]:
            send(functools.partial(ring_part, way, step), has_inv)

    def y_part(buf, chunk, send_sems, recv_sems, at, of, d):
        src = buf.at[chunk[0] : chunk[1], at_y(of)]
        return src, src, send_sems.at[at], recv_sems.at[at], {"pr": at_y(d)}

    def y_send(buf, chunks, send_sems, recv_sems, some, cond):
        for n in some:
            for way, d in ((0, 1), (1, -1)) if n % 2 == 0 else ((1, -1), (0, 1)):
                send(functools.partial(y_part, buf, chunks[n], send_sems, recv_sems, 3 * n + way, 0, d), cond)

    def y_landed(buf, chunks, send_sems, recv_sems, n, at, of, d):
        src, _, send_sem, recv_sem, device = y_part(buf, chunks[n], send_sems, recv_sems, at, of, -d)
        arrived(src, send_sem, recv_sem, device)

    def y_pass(buf, chunks, send_sems, recv_sems, some, cond):
        for n in some:
            d = 1 - 2 * (n % 2)
            y_landed(buf, chunks, send_sems, recv_sems, n, 3 * n + n % 2, -d, d)
            send(functools.partial(y_part, buf, chunks[n], send_sems, recv_sems, 3 * n + 2, -d, d), cond)

    def y_end_near(buf, chunks, send_sems, recv_sems):
        for n in range(len(chunks)):
            d = 1 - 2 * (n % 2)
            y_landed(buf, chunks, send_sems, recv_sems, n, 3 * n + 1 - n % 2, d, -d)

    def y_end_far(buf, chunks, send_sems, recv_sems):
        for n in range(len(chunks)):
            d = 1 - 2 * (n % 2)
            y_landed(buf, chunks, send_sems, recv_sems, n, 3 * n + 2, 2, d)

    def y_end(*gather):
        y_end_near(*gather)
        y_end_far(*gather)

    inv_chunks = ((0, 4), (4, 8), (8, 10), (10, 12), (12, 14), (14, 16))
    inv_y = (inv, inv_chunks, iy_send, iy_recv)

    near = (1, -1, 2, -2)
    order = (0, 1, -1, 2, -2, 5, -5, 6, 4, 7, 3, -6, -4, -7, -3, 8)
    chunks = ((0, 4), (4, 7), (7, 11), (11, 16))

    def hop(k, at, piece, d):
        return (
            piv.at[k, order.index(piece), y], piv.at[k, order.index(piece - d), y],
            g_send.at[k, at], g_recv.at[k, at], {"gz": at_z(d)},
        )

    def landed(k, at, piece, d):
        _, dst, send_sem, recv_sem, device = hop(k, at, piece, d)
        arrived(dst, send_sem, recv_sem, device)

    def piv_y(k):
        return pivots[k], chunks, y_sends[k], y_recvs[k]

    def gather_start(k, cond):
        for n, d in enumerate((5, -5)):
            send(functools.partial(hop, k, n, 0, d), cond)
        for n, d in enumerate(near):
            send(functools.partial(hop, k, 2 + n, 0, d), cond)

    def extra(k):
        return piv.at[k, 5 + core, y], piv.at[k, 15, y], g_send.at[k, 14], g_recv.at[k, 14], {"gz": at_z(-3 * sgn)}

    def gather_pass(k, cond):
        for n, d in enumerate((5, -5)):
            landed(k, n, 0, d)
            for m, e in enumerate(near):
                send(functools.partial(hop, k, 6 + 4 * n + m, -d, e), cond)
        send(functools.partial(extra, k), cond)
        for m, d in enumerate(near):
            landed(k, 2 + m, 0, d)
        y_send(*piv_y(k), (0, 1), cond)

    def gather_near(k, cond):
        for n, d in enumerate((5, -5)):
            for m, e in enumerate(near):
                landed(k, 6 + 4 * n + m, -d, e)
        _, dst, send_sem, recv_sem, device = extra(k)
        arrived(dst, send_sem, recv_sem, device)
        y_send(*piv_y(k), (2, 3), cond)

    def in_rows(j):
        return pl.ds(pl.multiple_of(SUB * at_z(order[j]), SUB), SUB)

    pivots = [piv.at[k] for k in range(PANELS)]
    y_sends = [py_send.at[k] for k in range(PANELS)]
    y_recvs = [py_recv.at[k] for k in range(PANELS)]

    for step in range(9):
        if step == 0:
            load_inv.wait()
        if step == 1:
            load.wait()
        @pl.when(has_inv())
        def _():
            for way in range(2):
                if step <= hops[way]:
                    ring_step(way, step)
            if step == 4:
                y_send(*inv_y, (0, 1), has_inv)
            if step == 6:
                y_pass(*inv_y, (0, 1), has_inv)
                y_send(*inv_y, (2, 3), has_inv)
            if step == 8:
                y_send(*inv_y, (4, 5), has_inv)

        for q in range(4):
            for way in range(2):
                if step <= hops[way]:
                    rs_step(q, way, step)
    for q in range(4):
        front[q] = rows_of(q, z)[...] + slots[q, 0, 7] + slots[q, 1, 6]

    def is_top():
        return y == 0

    def share(d):
        return (
            front.at[:, :, COLS * d : COLS * d + COLS], tops, a_send.at[d - 1], a_recv.at[0], {"pr": none + d},
        )

    @pl.when(is_top())
    def _():
        for d in range(1, NY):
            send(functools.partial(share, d), is_top)
        tops[...] = front[:, :, 0:COLS]

    @pl.when(has_inv())
    def _():
        y_pass(*inv_y, (2, 3, 4, 5), has_inv)

    @pl.when(low_rows)
    def _():
        arrived(tops, a_send.at[0], a_recv.at[0], {"pr": none})

    def deal_part(k):
        cols = pl.ds(pl.multiple_of(COLS * y, COLS), COLS)
        return (
            tops.at[k], dealt.at[zlo, :, cols], d_send.at[k], d_recv.at[zlo, y], {"gz": 4 * k + zhi, "pr": none},
        )

    def away(k):
        return jnp.logical_not(jnp.logical_and(y == 0, 4 * k + zhi == z))

    def deal(k):
        @pl.when(away(k))
        def _():
            send(functools.partial(deal_part, k), functools.partial(away, k))

        @pl.when(jnp.logical_not(away(k)))
        def _():
            dealt[zlo, :, 0:COLS] = tops[k]

    def owns(k):
        return c == k

    def right_of(k):
        return c > k

    def low_owns(k):
        return jnp.logical_and(c == k, y > 0)

    def peers_of(k):
        owner_x, owner_core = k // 2, k % 2
        same = [2 * n + owner_core for n in range(NC // 2) if n != owner_x and 2 * n + 1 > k]
        same[:2] = same[1::-1]
        if owner_core == 0:
            same.append(k + 1)
        if k == 1:
            same.append(2)
        return same

    def mult_ref(kind, k):
        if kind == 1:
            return mult.at[k]
        return top_mult.at[k, k + 2 : 4] if kind else top_mult.at[k, k + 1 : k + 2]

    def mult_part(kind, k, n, peer):
        ref = mult_ref(kind, k)
        return ref, ref, m_send.at[kind, k, n], m_recv.at[kind, k], {"pc": none + peer}

    def mult_on(kind, k):
        ref = mult_ref(kind, k)
        return ref, ref, m_send.at[kind, k, 0], m_recv.at[kind, k], {"pc": 2 * x + 1 - core}

    def hands_on(kind, k):
        given = jnp.logical_and(core == k % 2, jnp.logical_and(x != k // 2, c > k))
        if k == 1:
            given = jnp.logical_and(given, c > 3)
        return jnp.logical_and(given, y > 0) if kind == 1 else given

    def mult_in(kind, k):
        ref, _, send_sem, recv_sem, device = mult_on(kind, k)
        arrived(ref, send_sem, recv_sem, device)

    def take_on(kind, k):
        @pl.when(hands_on(kind, k))
        def _():
            mult_in(kind, k)
            send(functools.partial(mult_on, kind, k), functools.partial(hands_on, kind, k))

    def wait_mult(kind, k):
        pl.when(jnp.logical_not(hands_on(kind, k)))(lambda: mult_in(kind, k))

    def block_part(k, d):
        ref = blocks.at[y, k + 1 : 4]
        return ref, ref, a_send.at[2 + d], a_recv.at[d], {"pr": at_y(d)}

    def low_update(k, passing=False):
        def convert(m, d):
            for j in range(NZ):
                high, low = split(piv[k, j, at_y(d)])
                piv_hi[in_rows(j), COLS * m : COLS * m + COLS] = high
                piv_lo[in_rows(j), COLS * m : COLS * m + COLS] = low

        def subtract(m, pair):
            cols = slice(COLS * m, COLS * m + 2 * COLS)
            product = dot3(mult[k], piv_hi.at[:, cols], piv_lo.at[:, cols])
            for n, d in enumerate(pair):
                there = pl.ds(pl.multiple_of(COLS * at_y(d), COLS), COLS)
                part = product[:, COLS * n : COLS * n + COLS].reshape(4, SUB, COLS)
                front[:, :, there] = front[:, :, there] - part

        convert(0, 0)
        y_end_near(*piv_y(k))
        convert(1, 1)
        convert(2, -1)
        if passing:
            take_on(1, k)
        wait_mult(1, k)
        subtract(0, (0, 1))
        y_end_far(*piv_y(k))
        convert(3, 2)
        subtract(2, (-1, 2))

    def start(k):
        @pl.when(right_of(k))
        def _():
            piv[k, 0, y] = tops[k]
            gather_start(k, functools.partial(right_of, k))

    def exchange(k):
        @pl.when(owns(k))
        def _():
            blocks[y, k + 1 : 4] = tops[k + 1 : 4]
            for d in range(1, NY):
                send(functools.partial(block_part, k, d), functools.partial(owns, k))

    def top_update(k, first, end):
        rows = (end - first) * SUB
        product = dot3(top_mult[k, first:end].reshape(rows, NB), own_hi, own_lo)
        tops[first:end] = tops[first:end] - product.reshape(end - first, SUB, COLS)

    def panel(k):
        right = functools.partial(right_of, k)
        mine = functools.partial(owns, k)
        left = 3 - k

        if k >= 2:
            @pl.when(jnp.logical_and(c >= k, low_rows))
            def _():
                low_update(k - 2)

        pl.when(right())(lambda: gather_pass(k, right))
        deal(k)

        if k == 0:
            @pl.when(has_inv())
            def _():
                y_end(*inv_y)
                for way in range(2):
                    for step in range(way, hops[way] + 1):
                        source = at_z(sgn * (step if way else -step))
                        high, low = split(inv[ring_slot(way, step)].reshape(NY * 8, NB))
                        rows = pl.ds(pl.multiple_of(SUB * source, SUB), SUB)
                        inv_hi[rows, :] = high
                        inv_lo[rows, :] = low

        if k < 3:
            @pl.when(mine())
            def _():
                for d in range(1, NY):
                    arrived(blocks.at[at_y(-d), k + 1 : 4], a_send.at[2 + d], a_recv.at[d], {"pr": at_y(-d)})
                whole = jnp.concatenate([blocks[n, k + 1 : 4].reshape(left * SUB, COLS) for n in range(NY)], axis=1)
                top_mult[k, k + 1 : 4] = dot3(whole, inv_hi, inv_lo).reshape(left, SUB, NB)
                for kind in (0, 2) if k < 2 else (0,):
                    for n, peer in enumerate(peers_of(k)):
                        send(functools.partial(mult_part, kind, k, n, peer), mine)
                cols = pl.ds(pl.multiple_of(COLS * y, COLS), COLS)
                tops[k + 1 : 4] = top_mult[k, k + 1 : 4, :, cols]

        if k >= 1:
            @pl.when(right_of(k - 1))
            def _():
                y_pass(*piv_y(k - 1), range(4), functools.partial(right_of, k - 1))

            pl.when(low_owns(k))(lambda: low_update(k - 1))

        @pl.when(low_owns(k))
        def _():
            product = dot3(front[...].reshape(ROWS, NB), inv_hi, inv_lo)
            mult[k] = product
            for n, peer in enumerate(peers_of(k)):
                send(functools.partial(mult_part, 1, k, n, peer), functools.partial(low_owns, k))

        @pl.when(right())
        def _():
            if k < 3:
                take_on(0, k)
            if k == 3:
                take_on(1, k - 1)
            gather_near(k, right)
            if k == 3:
                y_pass(*piv_y(k), (0, 1), right)
                pl.when(low_rows)(lambda: low_update(k - 1))
            if k < 3:
                for j in range(NZ):
                    high, low = split(piv[k, j, y])
                    own_hi[in_rows(j), :] = high
                    own_lo[in_rows(j), :] = low
                wait_mult(0, k)
                top_update(k, k + 1, k + 2)

        if k < 3:
            start(k + 1)
        if k < 2:
            @pl.when(right())
            def _():
                take_on(2, k)
                wait_mult(2, k)
                top_update(k, k + 2, 4)

            exchange(k + 1)

        if k == 1 or k == 2:
            take_on(1, k - 1)

    start(0)
    exchange(0)
    for k in range(PANELS):
        panel(k)

    last = PANELS - 1

    @pl.when(right_of(last))
    def _():
        y_pass(*piv_y(last), (2, 3), functools.partial(right_of, last))
        pl.when(low_rows)(lambda: low_update(last, True))

    @pl.when(top)
    def _():
        for k in range(PANELS):
            @pl.when(right_of(k))
            def _():
                y_end(*piv_y(k))

    @pl.when(is_top())
    def _():
        for n in range(4):
            for m in range(NY):
                def from_far():
                    cols = slice(COLS * m, COLS * m + COLS)
                    arrived(dealt.at[n, :, cols], d_send.at[0], d_recv.at[n, m], {"gz": 4 * zlo + n, "pr": none + m})

                if m == 0:
                    pl.when(4 * zlo + n != z)(from_far)
                else:
                    from_far()
        out[...] = dealt[...].reshape(ROWS, NB)

    @pl.when(low_rows)
    def _():
        out[...] = front[...].reshape(ROWS, NB)

        for k in range(PANELS):
            @pl.when(owns(k))
            def _():
                out[...] = mult[k]

    for cond, copy in pending:
        if cond is None:
            copy().wait_send()
        else:
            pl.when(cond())(lambda: copy().wait_send())


def shards(contributions, pivot_inverses):
    f32, bf16 = jnp.float32, jnp.bfloat16
    dma = pltpu.SemaphoreType.DMA
    factored = pl.pallas_call(
        kernel,
        out_shape=jax.ShapeDtypeStruct((ROWS, NB), f32),
        in_specs=[pl.BlockSpec(memory_space=pl.ANY)] * 2,
        out_specs=pl.BlockSpec(memory_space=pltpu.VMEM),
        scratch_shapes=[
            pltpu.VMEM((NZ * ROWS, NB), f32),
            pltpu.VMEM((4, 2, 8, SUB, NB), f32),
            pltpu.VMEM((4, SUB, NB), f32),
            pltpu.VMEM((4, SUB, COLS), f32),
            pltpu.VMEM((NZ, NY, 8, NB), f32),
            pltpu.VMEM((PANELS, NZ, NY, SUB, COLS), f32),
            pltpu.VMEM((NB, NB), bf16),
            pltpu.VMEM((NB, NB), bf16),
            pltpu.VMEM((NB, COLS), bf16),
            pltpu.VMEM((NB, COLS), bf16),
            pltpu.VMEM((NB, NB), bf16),
            pltpu.VMEM((NB, NB), bf16),
            pltpu.VMEM((NY, 4, SUB, COLS), f32),
            pltpu.VMEM((PANELS, 4, SUB, NB), f32),
            pltpu.VMEM((PANELS, ROWS, NB), f32),
            pltpu.VMEM((4, SUB, NB), f32),
            dma((2,)),
            dma((4, 2, 8)),
            dma((4, 2, 8)),
            dma((2, 8)),
            dma((2, 8)),
            dma((18,)),
            dma((18,)),
            dma((PANELS, 15)),
            dma((PANELS, 15)),
            dma((PANELS, 12)),
            dma((PANELS, 12)),
            dma((6,)),
            dma((4,)),
            dma((3, PANELS, 5)),
            dma((3, PANELS)),
            dma((PANELS,)),
            dma((4, NY)),
        ],
        compiler_params=pltpu.CompilerParams(
            collective_id=0, has_side_effects=True, vmem_limit_bytes=56 * 1024 * 1024
        ),
    )(contributions[0], pivot_inverses)
    return factored[None]


def solution(mesh):
    placed = (P("gz", "pr", "pc"), P(None, ("gz", "pr"), None))
    return jax.shard_map(
        shards, mesh=mesh, in_specs=placed, out_specs=P("pr", "gz", "pc"), check_vma=False
    )
```
